32 devices in a mesh: ens: 2 (over x), lon: 16 (over z, y, core).
Axes of the slice: x: 2, y: 2, z: 4, core: 2. Of those that a mesh axis runs over, the one named last changes fastest.
Arguments:
- increment: float32 [4, 4, 128, 512], P(None, None, ('ens', 'lon')), parts along dimension 2, may hold values from -12 to 12
- coeffs: float32 [3, 4, 128, 512], P(None, None, ('ens', 'lon')), parts along dimension 2, may hold values from 0.02 to 0.3
- polar_rows: int32 [64], P('ens'), parts along dimension 0, may hold values from 0 to 511, as said below
- polar_weight: float32 [64], P('ens'), parts along dimension 0, may hold values from 0.2 to 0.8
- block_index: int32 [512], P(('ens', 'lon')), parts along dimension 0, may hold values from 0 to 63
- send_dest: int32 [512], P(('ens', 'lon')), parts along dimension 0, may hold values from 0 to 15, as said below
- slot_count: int32 [512], P(('ens', 'lon')), parts along dimension 0, may hold values from 0 to 2, as said below
- jacobian: float32 [1024, 8, 512], P(('ens', 'lon')), parts along dimension 0, may hold values from -2 to 2
- observed: float32 [1024, 8], P(('ens', 'lon')), parts along dimension 0, may hold values from -6 to 6
- obs_weight: float32 [1024, 8], P(('ens', 'lon')), parts along dimension 0, may hold values from 0.25 to 4
- bg_weight: float32 [4, 4], replicated, may hold values from 0.02 to 0.1
Outputs:
- gradient: float32 [4, 4, 128, 512], P(None, None, ('ens', 'lon')), parts along dimension 2
- model_state: float32 [4, 4, 128, 512], P(None, None, ('ens', 'lon')), parts along dimension 2
- obs_residual: float32 [1024, 8], P(('ens', 'lon')), parts along dimension 0
The draws below stay inside these ranges and needn't reach their ends.
There are 2 independent parts, one for each index of `ens`. The reference program is written for one: setup_inputs(seed, part) draws one part's arguments, and reference() takes and returns one part's arrays. A program takes and returns all parts, laid end to end along the dimension named above; an argument that names none is the same for every part. Nothing has to cross between parts.
Inputs may be any that keep to these rules, and one draw needn't show every extreme that they name: `polar_rows`: 32 distinct latitudes, half among the 32 lowest and half among the 32 highest. `send_dest`: each device sends exactly 16 blocks and at most 2 to one owner; some owner receives 2 from every device. `slot_count`: entry o * 16 + s counts the sends of device s to owner o.
All inputs are finite; a program needn't handle non-finite values.
Results may differ from the reference program's by a relative error of at most 0.0001.
Values sent between devices are 32-bit elements; how exact they have to be, the bound alone decides.
A program may use at most 128 MiB of HBM per device.

```python
import math
import jax
import jax.numpy as jnp
from jax import lax

TRACERS = 4
LEVELS = 4
LON_DEV = 4
LAT = 512
STEPS = 4
POLE = 32
OBS = 8
CAP = 2
LON = 64
BLOCKS = 64
SENDS = 16
OWNED = 32
SEND_ALL = 256
OWN_ALL = 512
N_LON = 16


def routing(key):
    base_key = jax.random.fold_in(key, 11)
    key_owner, key_holder, key_spread = jax.random.split(base_key, 3)
    owner_perm = jax.random.permutation(key_owner, N_LON).astype(jnp.int32)
    holder_perm = jax.random.permutation(key_holder, N_LON).astype(jnp.int32)
    spread = jax.random.randint(key_spread, ((N_LON - 2) // 2,), 0, N_LON + 1, dtype=jnp.int32)
    head_loads = jnp.array([OWNED, 0], dtype=jnp.int32)
    paired = jnp.stack([N_LON + spread, N_LON - spread], axis=1).reshape(-1)
    owner_loads = jnp.concatenate([head_loads, paired]).astype(jnp.int32)
    run_ends = jnp.cumsum(owner_loads).astype(jnp.int32)
    position = jnp.arange(SEND_ALL, dtype=jnp.int32)
    owner_rank = jnp.sum((run_ends[None, :] <= position[:, None]).astype(jnp.int32), axis=1)
    owner = owner_perm[owner_rank]
    holder = holder_perm[position % N_LON]
    send_slot = position // N_LON
    send_dest = jnp.zeros((N_LON, SENDS), jnp.int32).at[holder, send_slot].set(owner).reshape(-1)
    counts = jnp.zeros((N_LON, N_LON), jnp.int32).at[owner, holder].add(1).reshape(-1)
    return (send_dest, counts)


def draw_send_dest(key, part):
    return routing(key)[0]


def draw_slot_count(key, part):
    return routing(key)[1]


def draw_polar_rows(key, part):
    half_count = POLE // 2
    key_south, key_north = jax.random.split(jax.random.fold_in(key, 5))
    edge_row = jnp.zeros((1,), jnp.int32)
    south_rows = jnp.concatenate([edge_row, 1 + jax.random.permutation(key_south, POLE - 1)[:half_count - 1].astype(jnp.int32)])
    north_rows = LAT - 1 - jnp.concatenate([edge_row, 1 + jax.random.permutation(key_north, POLE - 1)[:half_count - 1].astype(jnp.int32)])
    return jnp.concatenate([south_rows, north_rows]).astype(jnp.int32)


def draw_increment(key, part):
    full_shape = (TRACERS, LEVELS, LON, LAT)
    lon_ramp = (1.0 + 2.0 * jnp.arange(LON, dtype=jnp.float32) / max(LON - 1, 1))[None, None, :, None]
    return jax.random.truncated_normal(key, -4.0, 4.0, full_shape, jnp.float32) * lon_ramp


def obs_pattern(key):
    order = jax.random.permutation(jax.random.fold_in(key, 23), OBS).astype(jnp.int32)
    return jnp.where(order < OBS // 2, 1.0, -1.0).astype(jnp.float32)


def draw_jacobian(key, part):
    key_noise, key_mag, key_sign = jax.random.split(jax.random.fold_in(key, 31), 3)
    pattern = obs_pattern(key)
    sign_cells = jnp.where(jax.random.randint(key_sign, (LAT,), 0, 2) == 0, -1.0, 1.0).astype(jnp.float32)
    sender = (jnp.arange(OWN_ALL, dtype=jnp.int32) % OWNED // CAP).astype(jnp.float32)
    full_shape = (OWN_ALL, OBS, LAT)
    noise = jax.random.truncated_normal(key_noise, -4.0, 4.0, full_shape, jnp.float32)
    ramp = 1.0 + 2.0 * sender / max(N_LON - 1, 1)
    profile = sign_cells * jax.random.uniform(key_mag, (LAT,), jnp.float32, 0.5, 1.5)
    shared = 0.5 * ramp[:, None, None] * pattern[None, :, None] * profile[None, None, :]
    return (noise + shared) * LAT ** (-0.5)


def draw_observed(key, part):
    key_noise = jax.random.fold_in(key, 37)
    pattern = obs_pattern(key)
    full_shape = (OWN_ALL, OBS)
    noise = jax.random.truncated_normal(key_noise, -4.0, 4.0, full_shape, jnp.float32)
    return noise + 2.0 * pattern[None, :]


def with_ends(drawn, key, low, largest):
    longest = drawn.shape.index(max(drawn.shape))
    spots = []
    for shift in (0, 1):
        where = [jax.random.randint(jax.random.fold_in(key, axis), (), 0, length) for axis, length in enumerate(drawn.shape)]
        where[longest] = (where[longest] + shift) % drawn.shape[longest]
        spots.append(tuple(where))
    return drawn.at[spots[0]].set(low).at[spots[1]].set(largest)


def block_scale(key, dims, pieces, low, high):
    gain, own = 1.0, jax.random.fold_in(key, 6)
    for axis_at, parts in pieces:
        steps = jnp.exp(jax.random.uniform(jax.random.fold_in(own, axis_at), (parts,), jnp.float32, low / len(pieces), high / len(pieces)))
        gain = gain * jnp.repeat(steps, dims[axis_at] // parts).reshape([-1 if axis == axis_at else 1 for axis in range(len(dims))])
    return gain


def setup_inputs(seed: int = 0, part: int = 0) -> dict:
    keys = jax.random.split(jax.random.key(seed), 12)
    part_splits = jax.random.split(jax.random.fold_in(keys[11], part), 12)
    return {
        "increment": draw_increment(jax.random.fold_in(jax.random.fold_in(keys[11], part), 71), part),
        "coeffs": jnp.clip(0.02 + 0.28 * jax.random.uniform(part_splits[1], (3, LEVELS, LON, LAT), jnp.float32) ** block_scale(part_splits[1], (3, LEVELS, LON, LAT), ((2, 16),), -0.2, 0.2), 0.02, 0.3),
        "polar_rows": draw_polar_rows(jax.random.fold_in(jax.random.fold_in(keys[11], part), 71), part),
        "polar_weight": jnp.clip(jax.random.uniform(part_splits[3], (POLE,), jnp.float32, 0.2, 0.8), 0.2, 0.8),
        "block_index": with_ends(jax.random.randint(part_splits[4], (SEND_ALL,), 0, BLOCKS), jax.random.fold_in(part_splits[4], 1), 0, BLOCKS - 1).astype(jnp.int32),
        "send_dest": draw_send_dest(jax.random.fold_in(jax.random.fold_in(keys[11], part), 71), part),
        "slot_count": draw_slot_count(jax.random.fold_in(jax.random.fold_in(keys[11], part), 71), part),
        "jacobian": draw_jacobian(jax.random.fold_in(jax.random.fold_in(keys[11], part), 71), part),
        "observed": draw_observed(jax.random.fold_in(jax.random.fold_in(keys[11], part), 71), part),
        "obs_weight": jnp.clip(jnp.exp(math.log(4.0) - 2.7725887 * jax.random.uniform(part_splits[9], (OWN_ALL, OBS), jnp.float32) ** block_scale(part_splits[9], (OWN_ALL, OBS), ((0, 16),), -0.2, 0.2)), 0.25, 4.0),
        "bg_weight": jnp.clip(jnp.exp(jax.random.uniform(keys[10], (TRACERS, LEVELS), jnp.float32, math.log(0.02), math.log(0.1))), 0.02, 0.1),
    }


def advance(field_in, coeffs):
    west_c, north_c, south_c = coeffs[0], coeffs[1], coeffs[2]
    zero_edge = jnp.zeros_like(field_in[..., :1])
    west_cells = jnp.roll(field_in, 1, axis=2)
    north_cells = jnp.concatenate([field_in[..., 1:], zero_edge], axis=3)
    south_cells = jnp.concatenate([zero_edge, field_in[..., :-1]], axis=3)
    return (1.0 - west_c - north_c - south_c) * field_in + west_c * west_cells + north_c * north_cells + south_c * south_cells


def retreat(adjoint_in, coeffs):
    west_c, north_c, south_c = coeffs[0], coeffs[1], coeffs[2]
    zero_edge = jnp.zeros_like(adjoint_in[..., :1])
    from_east = jnp.roll(west_c * adjoint_in, -1, axis=2)
    north_flux = north_c * adjoint_in
    south_flux = south_c * adjoint_in
    north_in = jnp.concatenate([zero_edge, north_flux[..., :-1]], axis=3)
    south_in = jnp.concatenate([south_flux[..., 1:], zero_edge], axis=3)
    return (1.0 - west_c - north_c - south_c) * adjoint_in + from_east + north_in + south_in


def polar_blend(field_in, polar_rows, polar_weight):
    polar_vals = field_in[..., polar_rows]
    zonal_mean = jnp.sum(polar_vals, axis=2) / LON
    blended = (1.0 - polar_weight) * polar_vals + polar_weight * zonal_mean[:, :, None, :]
    return field_in.at[..., polar_rows].set(blended)


def reference(increment, coeffs, polar_rows, polar_weight, block_index, send_dest, slot_count, jacobian, observed, obs_weight, bg_weight):
    model_state = increment
    for repeat in range(STEPS):
        model_state = polar_blend(advance(model_state, coeffs), polar_rows, polar_weight)
    blocks = model_state.reshape(TRACERS, LEVELS, N_LON, LON_DEV, LAT).transpose(2, 0, 1, 3, 4).reshape(N_LON, BLOCKS, LAT)
    holder = jnp.arange(SEND_ALL, dtype=jnp.int32) // SENDS
    sent_blocks = blocks[holder, block_index]
    dest_table = send_dest.reshape(N_LON, SENDS)
    same_dest = dest_table[:, :, None] == dest_table[:, None, :]
    position = jnp.arange(SENDS, dtype=jnp.int32)
    earlier = position[None, :] < position[:, None]
    rank_in = jnp.sum((same_dest & earlier[None]).astype(jnp.int32), axis=2).reshape(-1)
    slot_row = holder * CAP + rank_in
    received = jnp.zeros((N_LON, OWNED, LAT), jnp.float32).at[send_dest, slot_row].set(sent_blocks)
    tile_table = jacobian.reshape(N_LON, OWNED, OBS, LAT)
    model_obs = jnp.einsum("nsoc,nsc->nso", tile_table, received, precision=lax.Precision.HIGHEST)
    count_table = slot_count.reshape(N_LON, N_LON)
    live_mask = (jnp.arange(CAP, dtype=jnp.int32)[None, None, :] < count_table[:, :, None]).astype(jnp.float32)
    live_mask = live_mask.reshape(N_LON, OWNED, 1)
    weighted = obs_weight.reshape(N_LON, OWNED, OBS) * live_mask
    misfit = model_obs - observed.reshape(N_LON, OWNED, OBS)
    bias_term = jnp.sum(weighted * misfit, axis=(1, 2)) / (1.0 + jnp.sum(weighted, axis=(1, 2)))
    residual = weighted * (misfit - bias_term[:, None, None])
    returned = jnp.einsum("nsoc,nso->nsc", tile_table, residual, precision=lax.Precision.HIGHEST)
    contrib = returned[send_dest, slot_row]
    adjoint = jnp.zeros((N_LON, BLOCKS, LAT), jnp.float32).at[holder, block_index].add(contrib)
    adjoint = adjoint.reshape(N_LON, TRACERS, LEVELS, LON_DEV, LAT).transpose(1, 2, 0, 3, 4).reshape(TRACERS, LEVELS, LON, LAT)
    for repeat in range(STEPS):
        adjoint = retreat(polar_blend(adjoint, polar_rows, polar_weight), coeffs)
    gradient = bg_weight[:, :, None, None] * increment + adjoint
    return gradient, model_state, residual.reshape(OWN_ALL, OBS)
```

```python
import functools

import jax
import jax.numpy as jnp
from jax import lax
from jax.experimental import pallas as pl
from jax.experimental.pallas import tpu as pltpu
from jax.sharding import PartitionSpec as P

STEPS = 4
CAP = 2
LANES = 128
HALF = 64
MESH = pl.DeviceIdType.MESH
EXACT = lax.Precision.HIGHEST


def kernel(
    n,
    sizes,
    x_ref,
    c_ref,
    rows_ref,
    pw_ref,
    bi_ref,
    sd_ref,
    sc_ref,
    jac_hbm,
    obs_ref,
    ow_ref,
    bg_ref,
    grad_ref,
    ms_ref,
    res_ref,
    jac,
    xarr,
    xwest,
    cwest,
    ceast,
    coef,
    msg,
    pbuf,
    pcoef,
    mout,
    mbuf,
    xfin,
    blk_out,
    blk_in,
    ret_out,
    ret_in,
    garr,
    geast,
    gmsg,
    gbuf,
    amout,
    ambuf,
    send_sem,
    recv_sem,
    jac_sem,
):
    tl, cols, lat, levels, sends, poles, obs = sizes
    solvers = tl
    me = lax.axis_index("lon")
    east, west = lax.rem(me + 1, n), lax.rem(me + n - 1, n)

    def others(count, act):
        if count == n:
            def body(s, carry):
                act(lax.rem(me + s, n))
                return carry

            lax.fori_loop(1, n, body, 0)
        else:
            def body(j, carry):
                @pl.when(j != me)
                def _():
                    act(j)

                return carry

            lax.fori_loop(0, count, body, 0)

    def remote(src, dst, phase, device):
        return pltpu.make_async_remote_copy(
            src_ref=src,
            dst_ref=dst,
            send_sem=send_sem.at[phase],
            recv_sem=recv_sem.at[phase],
            device_id={"lon": device},
            device_id_type=MESH,
        )

    def wait_bytes(ref, sem):
        pltpu.make_async_copy(ref, ref, sem).wait()

    def is_solver():
        return me < solvers

    def when_solver(act):
        if solvers == n:
            act()
        else:
            pl.when(is_solver())(act)

    def wait_solver_sends(ref, sem):
        if solvers == n:
            wait_bytes(ref.at[pl.ds(0, n - 1)], sem)
        else:
            @pl.when(is_solver())
            def _():
                wait_bytes(ref.at[pl.ds(0, solvers - 1)], sem)

            @pl.when(jnp.logical_not(is_solver()))
            def _():
                wait_bytes(ref.at[pl.ds(0, solvers)], sem)

    jac_copy = pltpu.make_async_copy(jac_hbm, jac, jac_sem)
    jac_copy.start()

    barrier = pltpu.get_barrier_semaphore()
    others(
        n,
        lambda j: pl.semaphore_signal(
            barrier, inc=1, device_id={"lon": j}, device_id_type=MESH
        ),
    )

    lane = lax.broadcasted_iota(jnp.int32, (1, LANES), 1)
    south = lane < HALF

    def pack(first, last):
        return jnp.where(south, first, last)

    msg[:, 0:cols, :] = pack(x_ref[:, :, 0:LANES], x_ref[:, :, lat - LANES : lat])
    for kind in range(3):
        part = pack(c_ref[kind, :, :, 0:LANES], c_ref[kind, :, :, lat - LANES : lat])
        lo = cols * (kind + 1)
        for t in range(tl // levels):
            msg[t * levels : (t + 1) * levels, lo : lo + cols, :] = part

    pl.semaphore_wait(barrier, n - 1)
    others(solvers, lambda j: remote(msg.at[j], pbuf.at[me], 0, j).start())

    for c in range(cols):
        xarr[c * tl : (c + 1) * tl, :] = x_ref[:, c, :]
    to_east = remote(xarr, xwest, 6, east)
    to_east.start()
    coef_east = remote(c_ref, cwest, 7, east)
    coef_east.start()
    coef_west = remote(c_ref, ceast, 8, west)
    coef_west.start()

    when_solver(lambda: pbuf.__setitem__((pl.ds(me, 1),), msg[pl.ds(me, 1)]))

    lat_row = lax.broadcasted_iota(jnp.int32, (1, lat), 1)
    weight = jnp.zeros((1, lat), jnp.float32)
    for p in range(poles):
        weight = jnp.where(lat_row == rows_ref[p], pw_ref[p], weight)
    w_first, w_last = weight[:, 0:LANES], weight[:, lat - LANES : lat]
    w_pack = pack(w_first, w_last)
    keep_pack = 1.0 - w_pack

    def edge_free(cn, cs, row, last):
        return jnp.where(row == last, 0.0, cn), jnp.where(row == 0, 0.0, cs)

    def arrange(src, base):
        for c in range(cols):
            cw, cn, cs = src[0, :, c, :], src[1, :, c, :], src[2, :, c, :]
            centre = 1.0 - cw - cn - cs
            cn, cs = edge_free(cn, cs, lat_row, lat - 1)
            for kind, value in enumerate((centre, cw, cn, cs)):
                coef[base + c, kind] = jnp.concatenate([value, value], axis=0)

    arrange(c_ref, cols)

    def routing(shape, owner_axis):
        owner = lax.broadcasted_iota(jnp.int32, shape, owner_axis)
        block = lax.broadcasted_iota(jnp.int32, shape, 1 - owner_axis)

        def body(k, carry):
            seen, first, second = carry
            index = bi_ref[k]
            row = lax.rem(index, cols) * tl + lax.div(index, cols)
            to_owner = owner == sd_ref[k]
            here = jnp.logical_and(to_owner, block == row)
            first = jnp.where(jnp.logical_and(here, seen == 0), 1.0, first)
            second = jnp.where(jnp.logical_and(here, seen == 1), 1.0, second)
            return jnp.where(to_owner, seen + 1, seen), first, second

        zero = jnp.zeros(shape, jnp.float32)
        init = (jnp.zeros(shape, jnp.int32), zero, zero)
        return lax.fori_loop(0, sends, body, init, unroll=sends <= 16)[1:]

    scatter_hot = routing((cols * tl, n), 1)
    gather_hot = routing((n, cols * tl), 0)

    eye = (
        lax.broadcasted_iota(jnp.int32, (obs, obs), 0)
        == lax.broadcasted_iota(jnp.int32, (obs, obs), 1)
    ).astype(jnp.float32)[None]
    slot_row = lax.broadcasted_iota(jnp.int32, (CAP * n, obs), 0)

    def live_body(d, live):
        mine = lax.div(slot_row, CAP) == d
        on = (lax.rem(slot_row, CAP) < sc_ref[d]).astype(jnp.float32)
        return jnp.where(mine, on, live)

    live = lax.fori_loop(
        0, n, live_body, jnp.zeros((CAP * n, obs), jnp.float32), unroll=n <= 16
    )

    def upright(flat):
        return jnp.sum(flat[:, None, :] * eye, axis=2, keepdims=True)

    weighted = upright(ow_ref[...] * live)
    observed = upright(obs_ref[...])
    weight_sum = 1.0 + jnp.sum(weighted, axis=(0, 1), keepdims=True)

    def solve_forward():
        wait_bytes(pbuf.at[pl.ds(0, n - 1)], recv_sem.at[0])
        v = [pbuf[:, c, :] for c in range(cols)]
        packs = []
        for c in range(cols):
            cw, cn, cs = (pbuf[:, cols * (k + 1) + c, :] for k in range(3))
            centre = 1.0 - cw - cn - cs
            cn, cs = edge_free(cn, cs, lane, LANES - 1)
            packs.append((centre, cw, cn, cs))
            for kind, value in enumerate(packs[c]):
                pcoef[c, kind] = value
        for step in range(STEPS):
            new = []
            for c in range(cols):
                centre, cw, cn, cs = packs[c]
                from_west = pltpu.roll(v[cols - 1], 1, 0) if c == 0 else v[c - 1]
                new.append(
                    centre * v[c]
                    + cw * from_west
                    + cn * pltpu.roll(v[c], LANES - 1, 1)
                    + cs * pltpu.roll(v[c], 1, 1)
                )
            total = sum(new[1:], new[0])
            mean = jnp.sum(total, axis=0, keepdims=True) / (cols * n)
            mout[step : step + 1, :] = mean
            v = [keep_pack * value + w_pack * mean for value in new]
        mbuf[pl.ds(me, 1)] = mout[...][None]
        others(n, lambda j: remote(mout, mbuf.at[me], 1, j).start())

    when_solver(solve_forward)

    coef_east.wait_recv()
    arrange(cwest, 0)
    coef_west.wait_recv()
    arrange(ceast, 2 * cols)
    to_east.wait_recv()
    wait_solver_sends(mbuf, recv_sem.at[1])

    def blend(value, first_mean, last_mean):
        middle = value[:, LANES : lat - LANES]
        first, last = value[:, 0:LANES], value[:, lat - LANES : lat]
        first = (1.0 - w_first) * first + w_first * first_mean
        last = (1.0 - w_last) * last + w_last * last_mean
        return jnp.concatenate([first, middle, last], axis=1)

    group = 2 * levels
    for h in range(tl // group):
        rows = slice(h * group, (h + 1) * group)
        at = lambda c: slice(c * tl + h * group, c * tl + (h + 1) * group)
        v = [xwest[at(c), :] for c in range(cols)] + [xarr[at(c), :] for c in range(cols)]
        for step in range(STEPS):
            mean = mbuf[rows, step, :]
            new = list(v)
            for c in range(step + 1, 2 * cols):
                value = (
                    coef[c, 0] * v[c]
                    + coef[c, 1] * v[c - 1]
                    + coef[c, 2] * pltpu.roll(v[c], lat - 1, 1)
                    + coef[c, 3] * pltpu.roll(v[c], 1, 1)
                )
                new[c] = blend(value, mean, mean)
            v = new
        for c in range(cols):
            xfin[at(c), :] = v[cols + c]
            ms_ref[rows, c, :] = v[cols + c]

    for r in range(CAP):
        blk_out[:, r, :] = jnp.dot(
            gather_hot[r], xfin[...], precision=EXACT, preferred_element_type=jnp.float32
        )
    others(n, lambda j: remote(blk_out.at[j], blk_in.at[me], 2, j).start())
    blk_in[pl.ds(me, 1)] = blk_out[pl.ds(me, 1)]
    jac_copy.wait()
    wait_bytes(blk_in.at[pl.ds(0, n - 1)], recv_sem.at[2])

    w4 = weighted.reshape(n, CAP, obs, 1)
    o4 = observed.reshape(n, CAP, obs, 1)
    misfit = []
    bias_sum = jnp.zeros((1, 1, 1), jnp.float32)
    for r in range(CAP):
        model = jnp.sum(jac[:, r] * blk_in[:, r : r + 1, :], axis=2, keepdims=True)
        misfit.append(model - o4[:, r])
        bias_sum += jnp.sum(w4[:, r] * misfit[r], axis=(0, 1), keepdims=True)
    bias = bias_sum / weight_sum
    residual = [w4[:, r] * (misfit[r] - bias) for r in range(CAP)]
    for r in range(CAP):
        ret_out[:, r : r + 1, :] = jnp.sum(jac[:, r] * residual[r], axis=1, keepdims=True)
    others(n, lambda j: remote(ret_out.at[j], ret_in.at[me], 3, j).start())
    ret_in[pl.ds(me, 1)] = ret_out[pl.ds(me, 1)]
    for r in range(CAP):
        res_ref[pl.ds(r, n, stride=CAP), :] = jnp.sum(residual[r] * eye, axis=1)
    wait_bytes(ret_in.at[pl.ds(0, n - 1)], recv_sem.at[3])

    start = jnp.dot(
        scatter_hot[0], ret_in[:, 0, :], precision=EXACT, preferred_element_type=jnp.float32
    )
    for r in range(1, CAP):
        start += jnp.dot(
            scatter_hot[r], ret_in[:, r, :], precision=EXACT, preferred_element_type=jnp.float32
        )
    garr[...] = start
    for c in range(cols):
        part = start[c * tl : (c + 1) * tl]
        gmsg[:, c, :] = pack(part[:, 0:LANES], part[:, lat - LANES : lat])
    others(solvers, lambda j: remote(gmsg.at[j], gbuf.at[me], 4, j).start())
    to_west = remote(garr, geast, 9, west)
    to_west.start()
    when_solver(lambda: gbuf.__setitem__((pl.ds(me, 1),), gmsg[pl.ds(me, 1)]))

    def solve_adjoint():
        wait_bytes(gbuf.at[pl.ds(0, n - 1)], recv_sem.at[4])
        g = [gbuf[:, c, :] for c in range(cols)]
        for step in range(STEPS):
            total = sum(g[1:], g[0])
            mean = jnp.sum(total, axis=0, keepdims=True) / (cols * n)
            amout[step : step + 1, :] = mean
            if step == STEPS - 1:
                break
            g = [keep_pack * value + w_pack * mean for value in g]
            flux = [pcoef[c, 1] * g[c] for c in range(cols)]
            new = []
            for c in range(cols):
                from_east = pltpu.roll(flux[0], n - 1, 0) if c == cols - 1 else flux[c + 1]
                new.append(
                    pcoef[c, 0] * g[c]
                    + from_east
                    + pltpu.roll(pcoef[c, 2] * g[c], 1, 1)
                    + pltpu.roll(pcoef[c, 3] * g[c], LANES - 1, 1)
                )
            g = new
        ambuf[pl.ds(me, 1)] = amout[...][None]
        others(n, lambda j: remote(amout, ambuf.at[me], 5, j).start())

    when_solver(solve_adjoint)
    to_west.wait_recv()
    wait_solver_sends(ambuf, recv_sem.at[5])

    group_row = lax.broadcasted_iota(jnp.int32, (group, 1), 0)
    for h in range(tl // group):
        rows = slice(h * group, (h + 1) * group)
        at = lambda c: slice(c * tl + h * group, c * tl + (h + 1) * group)
        g = [garr[at(c), :] for c in range(cols)] + [geast[at(c), :] for c in range(cols)]
        for step in range(STEPS):
            mean = ambuf[rows, step, :]
            last = 2 * cols - step
            g = [blend(value, mean, mean) for value in g[:last]]
            new = []
            for c in range(last - 1):
                k = cols + c
                new.append(
                    coef[k, 0] * g[c]
                    + coef[k + 1, 1] * g[c + 1]
                    + pltpu.roll(coef[k, 2] * g[c], 1, 1)
                    + pltpu.roll(coef[k, 3] * g[c], lat - 1, 1)
                )
            g = new
        background = jnp.zeros((group, 1), jnp.float32)
        for i in range(group):
            at_row = h * group + i
            value = bg_ref[at_row // levels, at_row % levels]
            background = jnp.where(group_row == i, value, background)
        for c in range(cols):
            grad_ref[rows, c, :] = background * xarr[at(c), :] + g[c]

    wait_solver_sends(msg, send_sem.at[0])
    wait_bytes(blk_out.at[pl.ds(0, n - 1)], send_sem.at[2])
    wait_bytes(ret_out.at[pl.ds(0, n - 1)], send_sem.at[3])
    wait_solver_sends(gmsg, send_sem.at[4])

    def drain_means():
        def body(s, carry):
            wait_bytes(mout, send_sem.at[1])
            wait_bytes(amout, send_sem.at[5])
            return carry

        lax.fori_loop(1, n, body, 0)

    when_solver(drain_means)
    to_east.wait_send()
    coef_east.wait_send()
    coef_west.wait_send()
    to_west.wait_send()


def shards(
    increment,
    coeffs,
    polar_rows,
    polar_weight,
    block_index,
    send_dest,
    slot_count,
    jacobian,
    observed,
    obs_weight,
    bg_weight,
):
    tracers, levels, cols, lat = increment.shape
    n = lax.axis_size("lon")
    tl = tracers * levels
    obs = jacobian.shape[1]
    sizes = (tl, cols, lat, levels, send_dest.shape[0], polar_rows.shape[0], obs)
    vmem = pl.BlockSpec(memory_space=pltpu.VMEM)
    smem = pl.BlockSpec(memory_space=pltpu.SMEM)
    f32 = jnp.float32
    field = jax.ShapeDtypeStruct((tl, cols, lat), f32)
    scratch = [
        pltpu.VMEM((n, CAP, obs, lat), f32),
        pltpu.VMEM((cols * tl, lat), f32),
        pltpu.VMEM((cols * tl, lat), f32),
        pltpu.VMEM(coeffs.shape, f32),
        pltpu.VMEM(coeffs.shape, f32),
        pltpu.VMEM((3 * cols, 4, 2 * levels, lat), f32),
        pltpu.VMEM((tl, 4 * cols, LANES), f32),
        pltpu.VMEM((n, 4 * cols, LANES), f32),
        pltpu.VMEM((cols, 4, n, LANES), f32),
        pltpu.VMEM((STEPS, LANES), f32),
        pltpu.VMEM((tl, STEPS, LANES), f32),
        pltpu.VMEM((cols * tl, lat), f32),
        pltpu.VMEM((n, CAP, lat), f32),
        pltpu.VMEM((n, CAP, lat), f32),
        pltpu.VMEM((n, CAP, lat), f32),
        pltpu.VMEM((n, CAP, lat), f32),
        pltpu.VMEM((cols * tl, lat), f32),
        pltpu.VMEM((cols * tl, lat), f32),
        pltpu.VMEM((tl, cols, LANES), f32),
        pltpu.VMEM((n, cols, LANES), f32),
        pltpu.VMEM((STEPS, LANES), f32),
        pltpu.VMEM((tl, STEPS, LANES), f32),
        pltpu.SemaphoreType.DMA((10,)),
        pltpu.SemaphoreType.DMA((10,)),
        pltpu.SemaphoreType.DMA,
    ]
    gradient, model_state, residual = pl.pallas_call(
        functools.partial(kernel, n, sizes),
        out_shape=(field, field, jax.ShapeDtypeStruct(observed.shape, f32)),
        in_specs=[vmem, vmem, smem, smem, smem, smem, smem, pl.BlockSpec(memory_space=pl.ANY), vmem, vmem, smem],
        out_specs=(vmem, vmem, vmem),
        scratch_shapes=scratch,
        compiler_params=pltpu.CompilerParams(
            collective_id=0, has_side_effects=True, vmem_limit_bytes=40 * 1024 * 1024
        ),
    )(
        increment.reshape(tl, cols, lat),
        coeffs,
        polar_rows,
        polar_weight,
        block_index,
        send_dest,
        slot_count,
        jacobian.reshape(n, CAP, obs, lat),
        observed,
        obs_weight,
        bg_weight,
    )
    return gradient.reshape(increment.shape), model_state.reshape(increment.shape), residual


def solution(mesh):
    placed = (
        P(None, None, ("ens", "lon"), None),
        P(None, None, ("ens", "lon"), None),
        P("ens"),
        P("ens"),
        P(("ens", "lon")),
        P(("ens", "lon")),
        P(("ens", "lon")),
        P(("ens", "lon"), None, None),
        P(("ens", "lon"), None),
        P(("ens", "lon"), None),
        P(),
    )
    return jax.shard_map(
        shards,
        mesh=mesh,
        in_specs=placed,
        out_specs=(
            P(None, None, ("ens", "lon"), None),
            P(None, None, ("ens", "lon"), None),
            P(("ens", "lon"), None),
        ),
        check_vma=False,
    )
```

```python
import functools

import jax
import jax.numpy as jnp
from jax import lax
from jax.experimental import pallas as pl
from jax.experimental.pallas import tpu as pltpu
from jax.sharding import PartitionSpec as P

STEPS = 4
CAP = 2
LANES = 128
HALF = 64
MESH = pl.DeviceIdType.MESH
EXACT = lax.Precision.HIGHEST


def kernel(
    n,
    sizes,
    x_hbm,
    c_hbm,
    rows_hbm,
    pw_hbm,
    bi_hbm,
    sd_hbm,
    sc_hbm,
    jac_hbm,
    obs_hbm,
    ow_hbm,
    bg_hbm,
    grad_ref,
    ms_ref,
    res_ref,
    x_ref,
    c_ref,
    rows_ref,
    pw_ref,
    bi_ref,
    sd_ref,
    sc_ref,
    jac,
    obs_ref,
    ow_ref,
    bg_ref,
    xarr,
    xwest,
    cwest,
    ceast,
    coef,
    msg,
    pbuf,
    pcoef,
    mout,
    mbuf,
    xfin,
    blk_out,
    blk_in,
    ret_out,
    ret_in,
    garr,
    geast,
    gmsg,
    gbuf,
    amout,
    ambuf,
    send_sem,
    recv_sem,
    load_sem,
):
    tl, cols, lat, levels, sends, poles, obs = sizes
    tracers = tl // levels
    spacing = n // levels
    me = lax.axis_index("lon")
    east, west = lax.rem(me + 1, n), lax.rem(me + n - 1, n)

    def others(act):
        def body(k, carry):
            act(lax.rem(me + k, n))
            return carry

        lax.fori_loop(1, n, body, 0, unroll=n <= 16)

    def to_solvers(act):
        for level in range(levels):
            @pl.when(me != level * spacing)
            def _():
                act(level, level * spacing)

    def remote(src, dst, phase, device):
        return pltpu.make_async_remote_copy(
            src_ref=src,
            dst_ref=dst,
            send_sem=send_sem.at[phase],
            recv_sem=recv_sem.at[phase],
            device_id={"lon": device},
            device_id_type=MESH,
        )

    def wait_bytes(ref, sem):
        pltpu.make_async_copy(ref, ref, sem).wait()

    solver = lax.rem(me, spacing) == 0
    level_here = lax.div(me, spacing)

    def wait_solver_blocks(ref, sem):
        @pl.when(solver)
        def _():
            wait_bytes(ref.at[pl.ds(0, levels - 1)], sem)

        @pl.when(jnp.logical_not(solver))
        def _():
            wait_bytes(ref, sem)

    pairs = (
        (x_hbm, x_ref),
        (c_hbm, c_ref),
        (rows_hbm, rows_ref),
        (pw_hbm, pw_ref),
        (bi_hbm, bi_ref),
        (sd_hbm, sd_ref),
        (sc_hbm, sc_ref),
        (obs_hbm, obs_ref),
        (ow_hbm, ow_ref),
        (bg_hbm, bg_ref),
        (jac_hbm, jac),
    )
    loads = [
        pltpu.make_async_copy(src, dst, load_sem.at[i]) for i, (src, dst) in enumerate(pairs)
    ]
    for load in loads:
        load.start()

    barrier = pltpu.get_barrier_semaphore()
    others(
        lambda j: pl.semaphore_signal(
            barrier, inc=1, device_id={"lon": j}, device_id_type=MESH
        ),
    )

    lane = lax.broadcasted_iota(jnp.int32, (1, LANES), 1)
    south = lane < HALF

    def pack(first, last):
        return jnp.where(south, first, last)

    loads[0].wait()
    for t in range(tracers):
        msg[:, t * cols : (t + 1) * cols, :] = pack(
            x_ref[t, :, :, 0:LANES], x_ref[t, :, :, lat - LANES : lat]
        )
    loads[1].wait()
    for kind in range(3):
        lo = (tracers + kind) * cols
        msg[:, lo : lo + cols, :] = pack(
            c_ref[kind, :, :, 0:LANES], c_ref[kind, :, :, lat - LANES : lat]
        )

    pl.semaphore_wait(barrier, n - 1)
    to_solvers(lambda level, j: remote(msg.at[level], pbuf.at[me], 0, j).start())

    for c in range(cols):
        for t in range(tracers):
            lo = c * tl + t * levels
            xarr[lo : lo + levels, :] = x_ref[t, :, c, :]
    to_east = remote(xarr, xwest, 6, east)
    to_east.start()
    coef_east = remote(c_ref, cwest, 7, east)
    coef_east.start()

    @pl.when(solver)
    def _():
        pbuf[pl.ds(me, 1)] = msg[pl.ds(level_here, 1)]

    loads[2].wait()
    loads[3].wait()

    lat_row = lax.broadcasted_iota(jnp.int32, (1, lat), 1)
    weight = jnp.zeros((1, lat), jnp.float32)
    for p in range(poles):
        weight = jnp.where(lat_row == rows_ref[p], pw_ref[p], weight)
    w_first, w_last = weight[:, 0:LANES], weight[:, lat - LANES : lat]
    w_pack = pack(w_first, w_last)
    keep_pack = 1.0 - w_pack

    def edge_free(cn, cs, row, last):
        return jnp.where(row == last, 0.0, cn), jnp.where(row == 0, 0.0, cs)

    def arrange(src, base):
        for c in range(cols):
            cw, cn, cs = src[0, :, c, :], src[1, :, c, :], src[2, :, c, :]
            centre = 1.0 - cw - cn - cs
            cn, cs = edge_free(cn, cs, lat_row, lat - 1)
            for kind, value in enumerate((centre, cw, cn, cs)):
                coef[base + c, kind] = jnp.concatenate([value, value], axis=0)

    def routing(shape, owner_axis):
        owner = lax.broadcasted_iota(jnp.int32, shape, owner_axis)
        block = lax.broadcasted_iota(jnp.int32, shape, 1 - owner_axis)

        def body(k, carry):
            seen, first, second = carry
            index = bi_ref[k]
            row = lax.rem(index, cols) * tl + lax.div(index, cols)
            to_owner = owner == sd_ref[k]
            here = jnp.logical_and(to_owner, block == row)
            first = jnp.where(jnp.logical_and(here, seen == 0), 1.0, first)
            second = jnp.where(jnp.logical_and(here, seen == 1), 1.0, second)
            return jnp.where(to_owner, seen + 1, seen), first, second

        zero = jnp.zeros(shape, jnp.float32)
        init = (jnp.zeros(shape, jnp.int32), zero, zero)
        return lax.fori_loop(0, sends, body, init, unroll=sends <= 16)[1:]

    @pl.when(solver)
    def _():
        wait_bytes(pbuf.at[pl.ds(0, n - 1)], recv_sem.at[0])
        v = [[pbuf[:, t * cols + c, :] for c in range(cols)] for t in range(tracers)]
        packs = []
        for c in range(cols):
            cw, cn, cs = (pbuf[:, (tracers + k) * cols + c, :] for k in range(3))
            centre = 1.0 - cw - cn - cs
            cn, cs = edge_free(cn, cs, lane, LANES - 1)
            packs.append((centre, cw, cn, cs))
            for kind, value in enumerate(packs[c]):
                pcoef[c, kind] = value
        for step in range(STEPS):
            for t in range(tracers):
                new = []
                for c in range(cols):
                    centre, cw, cn, cs = packs[c]
                    from_west = pltpu.roll(v[t][cols - 1], 1, 0) if c == 0 else v[t][c - 1]
                    new.append(
                        centre * v[t][c]
                        + cw * from_west
                        + cn * pltpu.roll(v[t][c], LANES - 1, 1)
                        + cs * pltpu.roll(v[t][c], 1, 1)
                    )
                total = sum(new[1:], new[0])
                mean = jnp.sum(total, axis=0, keepdims=True) / (cols * n)
                row = step * tracers + t
                mout[row : row + 1, :] = mean
                v[t] = [keep_pack * value + w_pack * mean for value in new]
        mbuf[pl.ds(level_here, 1)] = mout[...][None]
        others(lambda j: remote(mout, mbuf.at[level_here], 1, j).start())

    coef_west = remote(c_ref, ceast, 8, west)
    coef_west.start()
    arrange(c_ref, cols)
    loads[4].wait()
    loads[5].wait()
    gather_hot = routing((n, cols * tl), 0)
    coef_east.wait_recv()
    arrange(cwest, 0)
    to_east.wait_recv()
    wait_solver_blocks(mbuf, recv_sem.at[1])

    def means(buf, h, step):
        first = step * tracers + h * 2
        return jnp.concatenate([buf[:, first, :], buf[:, first + 1, :]], axis=0)

    def blend(value, first_mean, last_mean):
        middle = value[:, LANES : lat - LANES]
        first, last = value[:, 0:LANES], value[:, lat - LANES : lat]
        first = (1.0 - w_first) * first + w_first * first_mean
        last = (1.0 - w_last) * last + w_last * last_mean
        return jnp.concatenate([first, middle, last], axis=1)

    group = 2 * levels
    for h in range(tl // group):
        at = lambda c: slice(c * tl + h * group, c * tl + (h + 1) * group)
        v = [xwest[at(c), :] for c in range(cols)] + [xarr[at(c), :] for c in range(cols)]
        for step in range(STEPS):
            mean = means(mbuf, h, step)
            new = list(v)
            for c in range(step + 1, 2 * cols):
                value = (
                    coef[c, 0] * v[c]
                    + coef[c, 1] * v[c - 1]
                    + coef[c, 2] * pltpu.roll(v[c], lat - 1, 1)
                    + coef[c, 3] * pltpu.roll(v[c], 1, 1)
                )
                new[c] = blend(value, mean, mean)
            v = new
        for c in range(cols):
            xfin[at(c), :] = v[cols + c]
            for i in range(2):
                part = v[cols + c][i * levels : (i + 1) * levels]
                ms_ref[2 * h + i, :, c, :] = part

    for r in range(CAP):
        blk_out[:, r, :] = jnp.dot(
            gather_hot[r], xfin[...], precision=EXACT, preferred_element_type=jnp.float32
        )
    others(lambda j: remote(blk_out.at[j], blk_in.at[me], 2, j).start())
    blk_in[pl.ds(me, 1)] = blk_out[pl.ds(me, 1)]
    slots = CAP * n
    loads[6].wait()
    loads[7].wait()
    loads[8].wait()
    slot_lane = lax.broadcasted_iota(jnp.int32, (1, slots), 1)

    def live_body(d, live):
        mine = lax.div(slot_lane, CAP) == d
        on = (lax.rem(slot_lane, CAP) < sc_ref[d]).astype(jnp.float32)
        return jnp.where(mine, on, live)

    live = lax.fori_loop(
        0, n, live_body, jnp.zeros((1, slots), jnp.float32), unroll=n <= 16
    )
    slot_shape = (slots, 1, slots)
    eye = (
        lax.broadcasted_iota(jnp.int32, slot_shape, 0)
        == lax.broadcasted_iota(jnp.int32, slot_shape, 2)
    ).astype(jnp.float32)

    def upright(flat):
        return jnp.sum(flat[None] * eye, axis=2, keepdims=True)

    weighted = upright(ow_ref[...] * live)
    observed = upright(obs_ref[...])
    weight_sum = 1.0 + jnp.sum(weighted, axis=(0, 1), keepdims=True)
    coef_west.wait_recv()
    arrange(ceast, 2 * cols)
    loads[10].wait()
    wait_bytes(blk_in.at[pl.ds(0, n - 1)], recv_sem.at[2])

    w4 = weighted.reshape(n, CAP, obs, 1)
    o4 = observed.reshape(n, CAP, obs, 1)
    misfit = []
    bias_sum = jnp.zeros((1, 1, 1), jnp.float32)
    for r in range(CAP):
        model = jnp.sum(jac[:, r] * blk_in[:, r : r + 1, :], axis=2, keepdims=True)
        misfit.append(model - o4[:, r])
        bias_sum += jnp.sum(w4[:, r] * misfit[r], axis=(0, 1), keepdims=True)
    bias = bias_sum / weight_sum
    residual = [w4[:, r] * (misfit[r] - bias) for r in range(CAP)]
    for r in range(CAP):
        ret_out[:, r : r + 1, :] = jnp.sum(jac[:, r] * residual[r], axis=1, keepdims=True)
    others(lambda j: remote(ret_out.at[j], ret_in.at[me], 3, j).start())
    ret_in[pl.ds(me, 1)] = ret_out[pl.ds(me, 1)]
    both = jnp.stack(residual, axis=1).reshape(slots, obs, 1)
    res_ref[...] = jnp.sum(both * eye, axis=0)
    scatter_hot = routing((cols * tl, n), 1)
    wait_bytes(ret_in.at[pl.ds(0, n - 1)], recv_sem.at[3])

    start = jnp.dot(
        scatter_hot[0], ret_in[:, 0, :], precision=EXACT, preferred_element_type=jnp.float32
    )
    for r in range(1, CAP):
        start += jnp.dot(
            scatter_hot[r], ret_in[:, r, :], precision=EXACT, preferred_element_type=jnp.float32
        )
    garr[...] = start
    for c in range(cols):
        part = start[c * tl : (c + 1) * tl]
        polar = pack(part[:, 0:LANES], part[:, lat - LANES : lat])
        for t in range(tracers):
            gmsg[:, t * cols + c, :] = polar[t * levels : (t + 1) * levels]
    to_solvers(lambda level, j: remote(gmsg.at[level], gbuf.at[me], 4, j).start())
    to_west = remote(garr, geast, 9, west)
    to_west.start()

    @pl.when(solver)
    def _():
        gbuf[pl.ds(me, 1)] = gmsg[pl.ds(level_here, 1)]
        wait_bytes(gbuf.at[pl.ds(0, n - 1)], recv_sem.at[4])
        g = [[gbuf[:, t * cols + c, :] for c in range(cols)] for t in range(tracers)]
        for step in range(STEPS):
            for t in range(tracers):
                total = sum(g[t][1:], g[t][0])
                mean = jnp.sum(total, axis=0, keepdims=True) / (cols * n)
                row = step * tracers + t
                amout[row : row + 1, :] = mean
                if step == STEPS - 1:
                    continue
                part = [keep_pack * value + w_pack * mean for value in g[t]]
                flux = [pcoef[c, 1] * part[c] for c in range(cols)]
                new = []
                for c in range(cols):
                    from_east = pltpu.roll(flux[0], n - 1, 0) if c == cols - 1 else flux[c + 1]
                    new.append(
                        pcoef[c, 0] * part[c]
                        + from_east
                        + pltpu.roll(pcoef[c, 2] * part[c], 1, 1)
                        + pltpu.roll(pcoef[c, 3] * part[c], LANES - 1, 1)
                    )
                g[t] = new
        ambuf[pl.ds(level_here, 1)] = amout[...][None]
        others(lambda j: remote(amout, ambuf.at[level_here], 5, j).start())

    loads[9].wait()
    to_west.wait_recv()
    wait_solver_blocks(ambuf, recv_sem.at[5])

    group_row = lax.broadcasted_iota(jnp.int32, (group, 1), 0)
    for h in range(tl // group):
        at = lambda c: slice(c * tl + h * group, c * tl + (h + 1) * group)
        g = [garr[at(c), :] for c in range(cols)] + [geast[at(c), :] for c in range(cols)]
        for step in range(STEPS):
            mean = means(ambuf, h, step)
            last = 2 * cols - step
            g = [blend(value, mean, mean) for value in g[:last]]
            new = []
            for c in range(last - 1):
                k = cols + c
                new.append(
                    coef[k, 0] * g[c]
                    + coef[k + 1, 1] * g[c + 1]
                    + pltpu.roll(coef[k, 2] * g[c], 1, 1)
                    + pltpu.roll(coef[k, 3] * g[c], lat - 1, 1)
                )
            g = new
        background = jnp.zeros((group, 1), jnp.float32)
        for i in range(group):
            at_row = h * group + i
            value = bg_ref[at_row // levels, at_row % levels]
            background = jnp.where(group_row == i, value, background)
        for c in range(cols):
            value = background * xarr[at(c), :] + g[c]
            for i in range(2):
                grad_ref[2 * h + i, :, c, :] = value[i * levels : (i + 1) * levels]

    wait_solver_blocks(msg, send_sem.at[0])
    wait_bytes(blk_out.at[pl.ds(0, n - 1)], send_sem.at[2])
    wait_bytes(ret_out.at[pl.ds(0, n - 1)], send_sem.at[3])
    wait_solver_blocks(gmsg, send_sem.at[4])

    @pl.when(solver)
    def _():
        def body(s, carry):
            wait_bytes(mout, send_sem.at[1])
            wait_bytes(amout, send_sem.at[5])
            return carry

        lax.fori_loop(1, n, body, 0)

    to_east.wait_send()
    coef_east.wait_send()
    coef_west.wait_send()
    to_west.wait_send()


def shards(
    increment,
    coeffs,
    polar_rows,
    polar_weight,
    block_index,
    send_dest,
    slot_count,
    jacobian,
    observed,
    obs_weight,
    bg_weight,
):
    tracers, levels, cols, lat = increment.shape
    n = lax.axis_size("lon")
    tl = tracers * levels
    obs = jacobian.shape[1]
    sizes = (tl, cols, lat, levels, send_dest.shape[0], polar_rows.shape[0], obs)
    vmem = pl.BlockSpec(memory_space=pltpu.VMEM)
    hbm = pl.BlockSpec(memory_space=pltpu.HBM)
    f32, i32 = jnp.float32, jnp.int32
    field = jax.ShapeDtypeStruct(increment.shape, f32)
    flat = jax.ShapeDtypeStruct((obs, CAP * n), f32)
    rows = (tracers + 3) * cols
    scratch = [
        pltpu.VMEM(increment.shape, f32),
        pltpu.VMEM(coeffs.shape, f32),
        pltpu.SMEM(polar_rows.shape, i32),
        pltpu.SMEM(polar_weight.shape, f32),
        pltpu.SMEM(block_index.shape, i32),
        pltpu.SMEM(send_dest.shape, i32),
        pltpu.SMEM(slot_count.shape, i32),
        pltpu.VMEM((n, CAP, obs, lat), f32),
        pltpu.VMEM(flat.shape, f32),
        pltpu.VMEM(flat.shape, f32),
        pltpu.SMEM(bg_weight.shape, f32),
        pltpu.VMEM((cols * tl, lat), f32),
        pltpu.VMEM((cols * tl, lat), f32),
        pltpu.VMEM(coeffs.shape, f32),
        pltpu.VMEM(coeffs.shape, f32),
        pltpu.VMEM((3 * cols, 4, 2 * levels, lat), f32),
        pltpu.VMEM((levels, rows, LANES), f32),
        pltpu.VMEM((n, rows, LANES), f32),
        pltpu.VMEM((cols, 4, n, LANES), f32),
        pltpu.VMEM((STEPS * tracers, LANES), f32),
        pltpu.VMEM((levels, STEPS * tracers, LANES), f32),
        pltpu.VMEM((cols * tl, lat), f32),
        pltpu.VMEM((n, CAP, lat), f32),
        pltpu.VMEM((n, CAP, lat), f32),
        pltpu.VMEM((n, CAP, lat), f32),
        pltpu.VMEM((n, CAP, lat), f32),
        pltpu.VMEM((cols * tl, lat), f32),
        pltpu.VMEM((cols * tl, lat), f32),
        pltpu.VMEM((levels, tracers * cols, LANES), f32),
        pltpu.VMEM((n, tracers * cols, LANES), f32),
        pltpu.VMEM((STEPS * tracers, LANES), f32),
        pltpu.VMEM((levels, STEPS * tracers, LANES), f32),
        pltpu.SemaphoreType.DMA((10,)),
        pltpu.SemaphoreType.DMA((10,)),
        pltpu.SemaphoreType.DMA((11,)),
    ]
    gradient, model_state, residual = pl.pallas_call(
        functools.partial(kernel, n, sizes),
        out_shape=(field, field, flat),
        in_specs=[hbm] * 11,
        out_specs=(vmem, vmem, vmem),
        scratch_shapes=scratch,
        compiler_params=pltpu.CompilerParams(
            collective_id=0, has_side_effects=True, vmem_limit_bytes=62 * 1024 * 1024
        ),
    )(
        increment,
        coeffs,
        polar_rows,
        polar_weight,
        block_index,
        send_dest,
        slot_count,
        jacobian.reshape(n, CAP, obs, lat),
        observed.T,
        obs_weight.T,
        bg_weight,
    )
    return gradient, model_state, residual.T


def solution(mesh):
    placed = (
        P(None, None, ("ens", "lon"), None),
        P(None, None, ("ens", "lon"), None),
        P("ens"),
        P("ens"),
        P(("ens", "lon")),
        P(("ens", "lon")),
        P(("ens", "lon")),
        P(("ens", "lon"), None, None),
        P(("ens", "lon"), None),
        P(("ens", "lon"), None),
        P(),
    )
    return jax.shard_map(
        shards,
        mesh=mesh,
        in_specs=placed,
        out_specs=(
            P(None, None, ("ens", "lon"), None),
            P(None, None, ("ens", "lon"), None),
            P(("ens", "lon"), None),
        ),
        check_vma=False,
    )
```

```python
import functools

import jax
import jax.numpy as jnp
from jax import lax
from jax.experimental import pallas as pl
from jax.experimental.pallas import tpu as pltpu
from jax.sharding import PartitionSpec as P

STEPS = 4
CAP = 2
LANES = 128
HALF = 64
MESH = pl.DeviceIdType.MESH
EXACT = lax.Precision.HIGHEST


def kernel(
    n,
    sizes,
    x_hbm,
    c_hbm,
    rows_hbm,
    pw_hbm,
    bi_hbm,
    sd_hbm,
    sc_hbm,
    jac_hbm,
    obs_hbm,
    ow_hbm,
    bg_hbm,
    grad_ref,
    ms_ref,
    res_ref,
    x_ref,
    c_ref,
    rows_ref,
    pw_ref,
    bi_ref,
    sd_ref,
    sc_ref,
    jac,
    obs_ref,
    ow_ref,
    bg_ref,
    xarr,
    xwest,
    cwest,
    ceast,
    coef,
    msg,
    pbuf,
    pcoef,
    mout,
    mbuf,
    xfin,
    blk_out,
    blk_in,
    ret_out,
    ret_in,
    garr,
    geast,
    gmsg,
    gbuf,
    amout,
    ambuf,
    send_sem,
    recv_sem,
    load_sem,
):
    tl, cols, lat, levels, sends, poles, obs = sizes
    tracers = tl // levels
    spacing = n // levels
    me = lax.axis_index("lon")
    east, west = lax.rem(me + 1, n), lax.rem(me + n - 1, n)

    def others(act):
        def body(k, carry):
            act(lax.rem(me + k, n))
            return carry

        lax.fori_loop(1, n, body, 0, unroll=n <= 16)

    def to_solvers(act):
        for level in range(levels):
            @pl.when(me != level * spacing)
            def _():
                act(level, level * spacing)

    def remote(src, dst, phase, device):
        return pltpu.make_async_remote_copy(
            src_ref=src,
            dst_ref=dst,
            send_sem=send_sem.at[phase],
            recv_sem=recv_sem.at[phase],
            device_id={"lon": device},
            device_id_type=MESH,
        )

    def wait_bytes(ref, sem):
        pltpu.make_async_copy(ref, ref, sem).wait()

    solver = lax.rem(me, spacing) == 0
    level_here = lax.div(me, spacing)

    def wait_solver_blocks(ref, sem):
        @pl.when(solver)
        def _():
            wait_bytes(ref.at[pl.ds(0, levels - 1)], sem)

        @pl.when(jnp.logical_not(solver))
        def _():
            wait_bytes(ref, sem)

    pairs = (
        (x_hbm, x_ref),
        (c_hbm, c_ref),
        (rows_hbm, rows_ref),
        (pw_hbm, pw_ref),
        (bi_hbm, bi_ref),
        (sd_hbm, sd_ref),
        (sc_hbm, sc_ref),
        (obs_hbm, obs_ref),
        (ow_hbm, ow_ref),
        (bg_hbm, bg_ref),
        (jac_hbm, jac),
    )
    loads = [
        pltpu.make_async_copy(src, dst, load_sem.at[i]) for i, (src, dst) in enumerate(pairs)
    ]
    for load in loads:
        load.start()

    barrier = pltpu.get_barrier_semaphore()
    others(
        lambda j: pl.semaphore_signal(
            barrier, inc=1, device_id={"lon": j}, device_id_type=MESH
        ),
    )

    lane = lax.broadcasted_iota(jnp.int32, (1, LANES), 1)
    south = lane < HALF

    def pack(first, last):
        return jnp.where(south, first, last)

    loads[0].wait()
    for t in range(tracers):
        msg[:, t * cols : (t + 1) * cols, :] = pack(
            x_ref[t, :, :, 0:LANES], x_ref[t, :, :, lat - LANES : lat]
        )
    loads[1].wait()
    for kind in range(3):
        lo = (tracers + kind) * cols
        msg[:, lo : lo + cols, :] = pack(
            c_ref[kind, :, :, 0:LANES], c_ref[kind, :, :, lat - LANES : lat]
        )

    pl.semaphore_wait(barrier, n - 1)
    to_solvers(lambda level, j: remote(msg.at[level], pbuf.at[me], 0, j).start())

    for c in range(cols):
        for t in range(tracers):
            lo = c * tl + t * levels
            xarr[lo : lo + levels, :] = x_ref[t, :, c, :]
    to_east = remote(xarr, xwest, 6, east)
    to_east.start()
    coef_east = remote(c_ref, cwest, 7, east)
    coef_east.start()

    @pl.when(solver)
    def _():
        pbuf[pl.ds(me, 1)] = msg[pl.ds(level_here, 1)]

    loads[2].wait()
    loads[3].wait()

    lat_row = lax.broadcasted_iota(jnp.int32, (1, lat), 1)
    weight = jnp.zeros((1, lat), jnp.float32)
    for p in range(poles):
        weight = jnp.where(lat_row == rows_ref[p], pw_ref[p], weight)
    w_first, w_last = weight[:, 0:LANES], weight[:, lat - LANES : lat]
    w_pack = pack(w_first, w_last)
    keep_pack = 1.0 - w_pack

    def edge_free(cn, cs, row, last):
        return jnp.where(row == last, 0.0, cn), jnp.where(row == 0, 0.0, cs)

    def arrange(src, base):
        for c in range(cols):
            cw, cn, cs = src[0, :, c, :], src[1, :, c, :], src[2, :, c, :]
            centre = 1.0 - cw - cn - cs
            cn, cs = edge_free(cn, cs, lat_row, lat - 1)
            for kind, value in enumerate((centre, cw, cn, cs)):
                coef[base + c, kind] = jnp.concatenate([value, value], axis=0)

    def routing(shape, owner_axis):
        owner = lax.broadcasted_iota(jnp.int32, shape, owner_axis)
        block = lax.broadcasted_iota(jnp.int32, shape, 1 - owner_axis)

        def body(k, carry):
            seen, first, second = carry
            index = bi_ref[k]
            row = lax.rem(index, cols) * tl + lax.div(index, cols)
            to_owner = owner == sd_ref[k]
            here = jnp.logical_and(to_owner, block == row)
            first = jnp.where(jnp.logical_and(here, seen == 0), 1.0, first)
            second = jnp.where(jnp.logical_and(here, seen == 1), 1.0, second)
            return jnp.where(to_owner, seen + 1, seen), first, second

        zero = jnp.zeros(shape, jnp.float32)
        init = (jnp.zeros(shape, jnp.int32), zero, zero)
        return lax.fori_loop(0, sends, body, init, unroll=sends <= 16)[1:]

    @pl.when(solver)
    def _():
        wait_bytes(pbuf.at[pl.ds(0, n - 1)], recv_sem.at[0])
        v = [[pbuf[:, t * cols + c, :] for c in range(cols)] for t in range(tracers)]
        packs = []
        for c in range(cols):
            cw, cn, cs = (pbuf[:, (tracers + k) * cols + c, :] for k in range(3))
            centre = 1.0 - cw - cn - cs
            cn, cs = edge_free(cn, cs, lane, LANES - 1)
            packs.append((centre, cw, cn, cs))
            for kind, value in enumerate(packs[c]):
                pcoef[c, kind] = value
        for step in range(STEPS):
            for t in range(tracers):
                new = []
                for c in range(cols):
                    centre, cw, cn, cs = packs[c]
                    from_west = pltpu.roll(v[t][cols - 1], 1, 0) if c == 0 else v[t][c - 1]
                    new.append(
                        centre * v[t][c]
                        + cw * from_west
                        + cn * pltpu.roll(v[t][c], LANES - 1, 1)
                        + cs * pltpu.roll(v[t][c], 1, 1)
                    )
                total = sum(new[1:], new[0])
                mean = jnp.sum(total, axis=0, keepdims=True) / (cols * n)
                row = step * tracers + t
                mout[row : row + 1, :] = mean
                v[t] = [keep_pack * value + w_pack * mean for value in new]
        mbuf[pl.ds(level_here, 1)] = mout[...][None]
        others(lambda j: remote(mout, mbuf.at[level_here], 1, j).start())

    coef_west = remote(c_ref, ceast, 8, west)
    coef_west.start()
    arrange(c_ref, cols)
    loads[4].wait()
    loads[5].wait()
    gather_hot = routing((n, cols * tl), 0)
    coef_east.wait_recv()
    arrange(cwest, 0)
    to_east.wait_recv()
    wait_solver_blocks(mbuf, recv_sem.at[1])

    def means(buf, h, step):
        first = step * tracers + h * 2
        return jnp.concatenate([buf[:, first, :], buf[:, first + 1, :]], axis=0)

    def blend(value, first_mean, last_mean):
        middle = value[:, LANES : lat - LANES]
        first, last = value[:, 0:LANES], value[:, lat - LANES : lat]
        first = (1.0 - w_first) * first + w_first * first_mean
        last = (1.0 - w_last) * last + w_last * last_mean
        return jnp.concatenate([first, middle, last], axis=1)

    group = 2 * levels
    for h in range(tl // group):
        at = lambda c: slice(c * tl + h * group, c * tl + (h + 1) * group)
        v = [xwest[at(c), :] for c in range(cols)] + [xarr[at(c), :] for c in range(cols)]
        for step in range(STEPS):
            mean = means(mbuf, h, step)
            new = list(v)
            for c in range(step + 1, 2 * cols):
                value = (
                    coef[c, 0] * v[c]
                    + coef[c, 1] * v[c - 1]
                    + coef[c, 2] * pltpu.roll(v[c], lat - 1, 1)
                    + coef[c, 3] * pltpu.roll(v[c], 1, 1)
                )
                new[c] = blend(value, mean, mean)
            v = new
        for c in range(cols):
            xfin[at(c), :] = v[cols + c]
            for i in range(2):
                part = v[cols + c][i * levels : (i + 1) * levels]
                ms_ref[2 * h + i, :, c, :] = part

    for r in range(CAP):
        blk_out[:, r, :] = jnp.dot(
            gather_hot[r], xfin[...], precision=EXACT, preferred_element_type=jnp.float32
        )
    others(lambda j: remote(blk_out.at[j], blk_in.at[me], 2, j).start())
    blk_in[pl.ds(me, 1)] = blk_out[pl.ds(me, 1)]
    slots = CAP * n
    loads[6].wait()
    loads[7].wait()
    loads[8].wait()
    slot_lane = lax.broadcasted_iota(jnp.int32, (1, slots), 1)

    def live_body(d, live):
        mine = lax.div(slot_lane, CAP) == d
        on = (lax.rem(slot_lane, CAP) < sc_ref[d]).astype(jnp.float32)
        return jnp.where(mine, on, live)

    live = lax.fori_loop(
        0, n, live_body, jnp.zeros((1, slots), jnp.float32), unroll=n <= 16
    )
    slot_shape = (slots, 1, slots)
    eye = (
        lax.broadcasted_iota(jnp.int32, slot_shape, 0)
        == lax.broadcasted_iota(jnp.int32, slot_shape, 2)
    ).astype(jnp.float32)

    def upright(flat):
        return jnp.sum(flat[None] * eye, axis=2, keepdims=True)

    weighted = upright(ow_ref[...] * live)
    observed = upright(obs_ref[...])
    weight_sum = 1.0 + jnp.sum(weighted, axis=(0, 1), keepdims=True)
    coef_west.wait_recv()
    arrange(ceast, 2 * cols)
    loads[10].wait()
    wait_bytes(blk_in.at[pl.ds(0, n - 1)], recv_sem.at[2])

    w4 = weighted.reshape(n, CAP, obs, 1)
    o4 = observed.reshape(n, CAP, obs, 1)
    misfit = []
    bias_sum = jnp.zeros((1, 1, 1), jnp.float32)
    for r in range(CAP):
        model = jnp.sum(jac[:, r] * blk_in[:, r : r + 1, :], axis=2, keepdims=True)
        misfit.append(model - o4[:, r])
        bias_sum += jnp.sum(w4[:, r] * misfit[r], axis=(0, 1), keepdims=True)
    bias = bias_sum / weight_sum
    residual = [w4[:, r] * (misfit[r] - bias) for r in range(CAP)]
    for r in range(CAP):
        ret_out[:, r : r + 1, :] = jnp.sum(jac[:, r] * residual[r], axis=1, keepdims=True)
    others(lambda j: remote(ret_out.at[j], ret_in.at[me], 3, j).start())
    ret_in[pl.ds(me, 1)] = ret_out[pl.ds(me, 1)]
    both = jnp.stack(residual, axis=1).reshape(slots, obs, 1)
    res_ref[...] = jnp.sum(both * eye, axis=0)
    scatter_hot = routing((cols * tl, n), 1)
    wait_bytes(ret_in.at[pl.ds(0, n - 1)], recv_sem.at[3])

    start = jnp.dot(
        scatter_hot[0], ret_in[:, 0, :], precision=EXACT, preferred_element_type=jnp.float32
    )
    for r in range(1, CAP):
        start += jnp.dot(
            scatter_hot[r], ret_in[:, r, :], precision=EXACT, preferred_element_type=jnp.float32
        )
    garr[...] = start
    for c in range(cols):
        part = start[c * tl : (c + 1) * tl]
        polar = pack(part[:, 0:LANES], part[:, lat - LANES : lat])
        for t in range(tracers):
            gmsg[:, t * cols + c, :] = polar[t * levels : (t + 1) * levels]
    to_solvers(lambda level, j: remote(gmsg.at[level], gbuf.at[me], 4, j).start())
    to_west = remote(garr, geast, 9, west)
    to_west.start()

    @pl.when(solver)
    def _():
        gbuf[pl.ds(me, 1)] = gmsg[pl.ds(level_here, 1)]
        wait_bytes(gbuf.at[pl.ds(0, n - 1)], recv_sem.at[4])
        g = [[gbuf[:, t * cols + c, :] for c in range(cols)] for t in range(tracers)]
        for step in range(STEPS):
            for t in range(tracers):
                total = sum(g[t][1:], g[t][0])
                mean = jnp.sum(total, axis=0, keepdims=True) / (cols * n)
                row = step * tracers + t
                amout[row : row + 1, :] = mean
                if step == STEPS - 1:
                    continue
                part = [keep_pack * value + w_pack * mean for value in g[t]]
                flux = [pcoef[c, 1] * part[c] for c in range(cols)]
                new = []
                for c in range(cols):
                    from_east = pltpu.roll(flux[0], n - 1, 0) if c == cols - 1 else flux[c + 1]
                    new.append(
                        pcoef[c, 0] * part[c]
                        + from_east
                        + pltpu.roll(pcoef[c, 2] * part[c], 1, 1)
                        + pltpu.roll(pcoef[c, 3] * part[c], LANES - 1, 1)
                    )
                g[t] = new
        ambuf[pl.ds(level_here, 1)] = amout[...][None]
        others(lambda j: remote(amout, ambuf.at[level_here], 5, j).start())

    loads[9].wait()
    to_west.wait_recv()
    wait_solver_blocks(ambuf, recv_sem.at[5])

    group_row = lax.broadcasted_iota(jnp.int32, (group, 1), 0)
    for h in range(tl // group):
        at = lambda c: slice(c * tl + h * group, c * tl + (h + 1) * group)
        g = [garr[at(c), :] for c in range(cols)] + [geast[at(c), :] for c in range(cols)]
        for step in range(STEPS):
            mean = means(ambuf, h, step)
            last = 2 * cols - step
            g = [blend(value, mean, mean) for value in g[:last]]
            new = []
            for c in range(last - 1):
                k = cols + c
                new.append(
                    coef[k, 0] * g[c]
                    + coef[k + 1, 1] * g[c + 1]
                    + pltpu.roll(coef[k, 2] * g[c], 1, 1)
                    + pltpu.roll(coef[k, 3] * g[c], lat - 1, 1)
                )
            g = new
        background = jnp.zeros((group, 1), jnp.float32)
        for i in range(group):
            at_row = h * group + i
            value = bg_ref[at_row // levels, at_row % levels]
            background = jnp.where(group_row == i, value, background)
        for c in range(cols):
            value = background * xarr[at(c), :] + g[c]
            for i in range(2):
                grad_ref[2 * h + i, :, c, :] = value[i * levels : (i + 1) * levels]

    wait_solver_blocks(msg, send_sem.at[0])
    wait_bytes(blk_out.at[pl.ds(0, n - 1)], send_sem.at[2])
    wait_bytes(ret_out.at[pl.ds(0, n - 1)], send_sem.at[3])
    wait_solver_blocks(gmsg, send_sem.at[4])

    @pl.when(solver)
    def _():
        def body(s, carry):
            wait_bytes(mout, send_sem.at[1])
            wait_bytes(amout, send_sem.at[5])
            return carry

        lax.fori_loop(1, n, body, 0)

    to_east.wait_send()
    coef_east.wait_send()
    coef_west.wait_send()
    to_west.wait_send()


def store(*refs):
    sem = refs[6]
    copies = [pltpu.make_async_copy(refs[i], refs[i + 3], sem.at[i]) for i in range(3)]
    for copy in copies:
        copy.start()
    for copy in copies:
        copy.wait()


def shards(
    increment,
    coeffs,
    polar_rows,
    polar_weight,
    block_index,
    send_dest,
    slot_count,
    jacobian,
    observed,
    obs_weight,
    bg_weight,
):
    tracers, levels, cols, lat = increment.shape
    n = lax.axis_size("lon")
    tl = tracers * levels
    obs = jacobian.shape[1]
    sizes = (tl, cols, lat, levels, send_dest.shape[0], polar_rows.shape[0], obs)
    vmem = pl.BlockSpec(memory_space=pltpu.VMEM)
    hbm = pl.BlockSpec(memory_space=pltpu.HBM)
    f32, i32 = jnp.float32, jnp.int32
    field = jax.ShapeDtypeStruct(increment.shape, f32)
    flat = jax.ShapeDtypeStruct((obs, CAP * n), f32)
    rows = (tracers + 3) * cols
    scratch = [
        pltpu.VMEM(increment.shape, f32),
        pltpu.VMEM(coeffs.shape, f32),
        pltpu.SMEM(polar_rows.shape, i32),
        pltpu.SMEM(polar_weight.shape, f32),
        pltpu.SMEM(block_index.shape, i32),
        pltpu.SMEM(send_dest.shape, i32),
        pltpu.SMEM(slot_count.shape, i32),
        pltpu.VMEM((n, CAP, obs, lat), f32),
        pltpu.VMEM(flat.shape, f32),
        pltpu.VMEM(flat.shape, f32),
        pltpu.SMEM(bg_weight.shape, f32),
        pltpu.VMEM((cols * tl, lat), f32),
        pltpu.VMEM((cols * tl, lat), f32),
        pltpu.VMEM(coeffs.shape, f32),
        pltpu.VMEM(coeffs.shape, f32),
        pltpu.VMEM((3 * cols, 4, 2 * levels, lat), f32),
        pltpu.VMEM((levels, rows, LANES), f32),
        pltpu.VMEM((n, rows, LANES), f32),
        pltpu.VMEM((cols, 4, n, LANES), f32),
        pltpu.VMEM((STEPS * tracers, LANES), f32),
        pltpu.VMEM((levels, STEPS * tracers, LANES), f32),
        pltpu.VMEM((cols * tl, lat), f32),
        pltpu.VMEM((n, CAP, lat), f32),
        pltpu.VMEM((n, CAP, lat), f32),
        pltpu.VMEM((n, CAP, lat), f32),
        pltpu.VMEM((n, CAP, lat), f32),
        pltpu.VMEM((cols * tl, lat), f32),
        pltpu.VMEM((cols * tl, lat), f32),
        pltpu.VMEM((levels, tracers * cols, LANES), f32),
        pltpu.VMEM((n, tracers * cols, LANES), f32),
        pltpu.VMEM((STEPS * tracers, LANES), f32),
        pltpu.VMEM((levels, STEPS * tracers, LANES), f32),
        pltpu.SemaphoreType.DMA((10,)),
        pltpu.SemaphoreType.DMA((10,)),
        pltpu.SemaphoreType.DMA((11,)),
    ]
    gradient, model_state, residual = pl.pallas_call(
        functools.partial(kernel, n, sizes),
        out_shape=(field, field, flat),
        in_specs=[hbm] * 11,
        out_specs=(vmem, vmem, vmem),
        scratch_shapes=scratch,
        compiler_params=pltpu.CompilerParams(
            collective_id=0, has_side_effects=True, vmem_limit_bytes=62 * 1024 * 1024
        ),
    )(
        increment,
        coeffs,
        polar_rows,
        polar_weight,
        block_index,
        send_dest,
        slot_count,
        jacobian.reshape(n, CAP, obs, lat),
        observed.T,
        obs_weight.T,
        bg_weight,
    )
    gradient, model_state, residual = pl.pallas_call(
        store,
        out_shape=(field, field, flat),
        in_specs=[hbm] * 3,
        out_specs=(vmem, vmem, vmem),
        scratch_shapes=[pltpu.SemaphoreType.DMA((3,))],
    )(gradient, model_state, residual)
    return gradient, model_state, residual.T


def solution(mesh):
    placed = (
        P(None, None, ("ens", "lon"), None),
        P(None, None, ("ens", "lon"), None),
        P("ens"),
        P("ens"),
        P(("ens", "lon")),
        P(("ens", "lon")),
        P(("ens", "lon")),
        P(("ens", "lon"), None, None),
        P(("ens", "lon"), None),
        P(("ens", "lon"), None),
        P(),
    )
    return jax.shard_map(
        shards,
        mesh=mesh,
        in_specs=placed,
        out_specs=(
            P(None, None, ("ens", "lon"), None),
            P(None, None, ("ens", "lon"), None),
            P(("ens", "lon"), None),
        ),
        check_vma=False,
    )
```

```python
import functools

import jax
import jax.numpy as jnp
from jax import lax
from jax.experimental import pallas as pl
from jax.experimental.pallas import tpu as pltpu
from jax.sharding import PartitionSpec as P

STEPS = 4
CAP = 2
LANES = 128
HALF = 64
MESH = pl.DeviceIdType.MESH
EXACT = lax.Precision.HIGHEST


def kernel(
    n,
    sizes,
    x_hbm,
    c_hbm,
    rows_hbm,
    pw_hbm,
    bi_hbm,
    sd_hbm,
    sc_hbm,
    jac_hbm,
    obs_hbm,
    ow_hbm,
    bg_hbm,
    grad_ref,
    ms_ref,
    res_ref,
    x_ref,
    c_ref,
    rows_ref,
    pw_ref,
    bi_ref,
    sd_ref,
    sc_ref,
    jac,
    obs_ref,
    ow_ref,
    bg_ref,
    xarr,
    xwest,
    cwest,
    ceast,
    coef,
    msg,
    pbuf,
    pcoef,
    mout,
    mbuf,
    xfin,
    blk_out,
    blk_in,
    ret_out,
    ret_in,
    garr,
    geast,
    gmsg,
    gbuf,
    amout,
    ambuf,
    send_sem,
    recv_sem,
    load_sem,
):
    tl, cols, lat, levels, sends, poles, obs = sizes
    tracers = tl // levels
    spacing, nearest = n // (2 * levels), n // 4
    me = lax.axis_index("lon")
    east, west = lax.rem(me + 1, n), lax.rem(me + n - 1, n)

    def others(act):
        def body(k, carry):
            act(lax.rem(me + k, n))
            return carry

        lax.fori_loop(1, n, body, 0, unroll=n <= 16)

    def to_solvers(act):
        for level in range(levels):
            @pl.when(me != nearest + level * spacing)
            def _():
                act(level, nearest + level * spacing)

    def remote(src, dst, phase, device):
        return pltpu.make_async_remote_copy(
            src_ref=src,
            dst_ref=dst,
            send_sem=send_sem.at[phase],
            recv_sem=recv_sem.at[phase],
            device_id={"lon": device},
            device_id_type=MESH,
        )

    def wait_bytes(ref, sem):
        pltpu.make_async_copy(ref, ref, sem).wait()

    solver = functools.reduce(
        jnp.logical_or, [me == nearest + level * spacing for level in range(levels)]
    )
    level_here = lax.div(me - nearest, spacing)

    def wait_solver_blocks(ref, sem):
        @pl.when(solver)
        def _():
            wait_bytes(ref.at[pl.ds(0, levels - 1)], sem)

        @pl.when(jnp.logical_not(solver))
        def _():
            wait_bytes(ref, sem)

    pairs = (
        (x_hbm, x_ref),
        (c_hbm, c_ref),
        (rows_hbm, rows_ref),
        (pw_hbm, pw_ref),
        (bi_hbm, bi_ref),
        (sd_hbm, sd_ref),
        (sc_hbm, sc_ref),
        (obs_hbm, obs_ref),
        (ow_hbm, ow_ref),
        (bg_hbm, bg_ref),
        (jac_hbm, jac),
    )
    loads = [
        pltpu.make_async_copy(src, dst, load_sem.at[i]) for i, (src, dst) in enumerate(pairs)
    ]
    for load in loads:
        load.start()

    barrier = pltpu.get_barrier_semaphore()
    others(
        lambda j: pl.semaphore_signal(
            barrier, inc=1, device_id={"lon": j}, device_id_type=MESH
        ),
    )

    lane = lax.broadcasted_iota(jnp.int32, (1, LANES), 1)
    south = lane < HALF

    def pack(first, last):
        return jnp.where(south, first, last)

    loads[0].wait()
    for t in range(tracers):
        msg[:, t * cols : (t + 1) * cols, :] = pack(
            x_ref[t, :, :, 0:LANES], x_ref[t, :, :, lat - LANES : lat]
        )
    loads[1].wait()
    for kind in range(3):
        lo = (tracers + kind) * cols
        msg[:, lo : lo + cols, :] = pack(
            c_ref[kind, :, :, 0:LANES], c_ref[kind, :, :, lat - LANES : lat]
        )

    pl.semaphore_wait(barrier, n - 1)
    to_solvers(lambda level, j: remote(msg.at[level], pbuf.at[me], 0, j).start())

    for c in range(cols):
        for t in range(tracers):
            lo = c * tl + t * levels
            xarr[lo : lo + levels, :] = x_ref[t, :, c, :]
    to_east = remote(xarr, xwest, 6, east)
    to_east.start()
    coef_east = remote(c_ref, cwest, 7, east)
    coef_east.start()

    @pl.when(solver)
    def _():
        pbuf[pl.ds(me, 1)] = msg[pl.ds(level_here, 1)]

    loads[2].wait()
    loads[3].wait()

    lat_row = lax.broadcasted_iota(jnp.int32, (1, lat), 1)
    weight = jnp.zeros((1, lat), jnp.float32)
    for p in range(poles):
        weight = jnp.where(lat_row == rows_ref[p], pw_ref[p], weight)
    w_first, w_last = weight[:, 0:LANES], weight[:, lat - LANES : lat]
    w_pack = pack(w_first, w_last)
    keep_pack = 1.0 - w_pack

    def edge_free(cn, cs, row, last):
        return jnp.where(row == last, 0.0, cn), jnp.where(row == 0, 0.0, cs)

    def arrange(src, base):
        for c in range(cols):
            cw, cn, cs = src[0, :, c, :], src[1, :, c, :], src[2, :, c, :]
            centre = 1.0 - cw - cn - cs
            cn, cs = edge_free(cn, cs, lat_row, lat - 1)
            for kind, value in enumerate((centre, cw, cn, cs)):
                coef[base + c, kind] = jnp.concatenate([value, value], axis=0)

    def routing(shape, owner_axis):
        owner = lax.broadcasted_iota(jnp.int32, shape, owner_axis)
        block = lax.broadcasted_iota(jnp.int32, shape, 1 - owner_axis)

        def body(k, carry):
            seen, first, second = carry
            index = bi_ref[k]
            row = lax.rem(index, cols) * tl + lax.div(index, cols)
            to_owner = owner == sd_ref[k]
            here = jnp.logical_and(to_owner, block == row)
            first = jnp.where(jnp.logical_and(here, seen == 0), 1.0, first)
            second = jnp.where(jnp.logical_and(here, seen == 1), 1.0, second)
            return jnp.where(to_owner, seen + 1, seen), first, second

        zero = jnp.zeros(shape, jnp.float32)
        init = (jnp.zeros(shape, jnp.int32), zero, zero)
        return lax.fori_loop(0, sends, body, init, unroll=sends <= 16)[1:]

    @pl.when(solver)
    def _():
        wait_bytes(pbuf.at[pl.ds(0, n - 1)], recv_sem.at[0])
        v = [[pbuf[:, t * cols + c, :] for c in range(cols)] for t in range(tracers)]
        packs = []
        for c in range(cols):
            cw, cn, cs = (pbuf[:, (tracers + k) * cols + c, :] for k in range(3))
            centre = 1.0 - cw - cn - cs
            cn, cs = edge_free(cn, cs, lane, LANES - 1)
            packs.append((centre, cw, cn, cs))
            for kind, value in enumerate(packs[c]):
                pcoef[c, kind] = value
        for step in range(STEPS):
            for t in range(tracers):
                new = []
                for c in range(cols):
                    centre, cw, cn, cs = packs[c]
                    from_west = pltpu.roll(v[t][cols - 1], 1, 0) if c == 0 else v[t][c - 1]
                    new.append(
                        centre * v[t][c]
                        + cw * from_west
                        + cn * pltpu.roll(v[t][c], LANES - 1, 1)
                        + cs * pltpu.roll(v[t][c], 1, 1)
                    )
                total = sum(new[1:], new[0])
                mean = jnp.sum(total, axis=0, keepdims=True) / (cols * n)
                row = step * tracers + t
                mout[row : row + 1, :] = mean
                v[t] = [keep_pack * value + w_pack * mean for value in new]
        mbuf[pl.ds(level_here, 1)] = mout[...][None]
        others(lambda j: remote(mout, mbuf.at[level_here], 1, j).start())

    coef_west = remote(c_ref, ceast, 8, west)
    coef_west.start()
    arrange(c_ref, cols)
    loads[4].wait()
    loads[5].wait()
    gather_hot = routing((n, cols * tl), 0)
    coef_east.wait_recv()
    arrange(cwest, 0)
    to_east.wait_recv()
    wait_solver_blocks(mbuf, recv_sem.at[1])

    def means(buf, h, step):
        first = step * tracers + h * 2
        return jnp.concatenate([buf[:, first, :], buf[:, first + 1, :]], axis=0)

    def blend(value, first_mean, last_mean):
        middle = value[:, LANES : lat - LANES]
        first, last = value[:, 0:LANES], value[:, lat - LANES : lat]
        first = (1.0 - w_first) * first + w_first * first_mean
        last = (1.0 - w_last) * last + w_last * last_mean
        return jnp.concatenate([first, middle, last], axis=1)

    group = 2 * levels
    for h in range(tl // group):
        at = lambda c: slice(c * tl + h * group, c * tl + (h + 1) * group)
        v = [xwest[at(c), :] for c in range(cols)] + [xarr[at(c), :] for c in range(cols)]
        for step in range(STEPS):
            mean = means(mbuf, h, step)
            new = list(v)
            for c in range(step + 1, 2 * cols):
                value = (
                    coef[c, 0] * v[c]
                    + coef[c, 1] * v[c - 1]
                    + coef[c, 2] * pltpu.roll(v[c], lat - 1, 1)
                    + coef[c, 3] * pltpu.roll(v[c], 1, 1)
                )
                new[c] = blend(value, mean, mean)
            v = new
        for c in range(cols):
            xfin[at(c), :] = v[cols + c]
            for i in range(2):
                part = v[cols + c][i * levels : (i + 1) * levels]
                ms_ref[2 * h + i, :, c, :] = part

    for r in range(CAP):
        blk_out[:, r, :] = jnp.dot(
            gather_hot[r], xfin[...], precision=EXACT, preferred_element_type=jnp.float32
        )
    others(lambda j: remote(blk_out.at[j], blk_in.at[me], 2, j).start())
    blk_in[pl.ds(me, 1)] = blk_out[pl.ds(me, 1)]
    slots = CAP * n
    loads[6].wait()
    loads[7].wait()
    loads[8].wait()
    slot_lane = lax.broadcasted_iota(jnp.int32, (1, slots), 1)

    def live_body(d, live):
        mine = lax.div(slot_lane, CAP) == d
        on = (lax.rem(slot_lane, CAP) < sc_ref[d]).astype(jnp.float32)
        return jnp.where(mine, on, live)

    live = lax.fori_loop(
        0, n, live_body, jnp.zeros((1, slots), jnp.float32), unroll=n <= 16
    )
    slot_shape = (slots, 1, slots)
    eye = (
        lax.broadcasted_iota(jnp.int32, slot_shape, 0)
        == lax.broadcasted_iota(jnp.int32, slot_shape, 2)
    ).astype(jnp.float32)

    def upright(flat):
        return jnp.sum(flat[None] * eye, axis=2, keepdims=True)

    weighted = upright(ow_ref[...] * live)
    observed = upright(obs_ref[...])
    weight_sum = 1.0 + jnp.sum(weighted, axis=(0, 1), keepdims=True)
    coef_west.wait_recv()
    arrange(ceast, 2 * cols)
    loads[10].wait()
    wait_bytes(blk_in.at[pl.ds(0, n - 1)], recv_sem.at[2])

    w4 = weighted.reshape(n, CAP, obs, 1)
    o4 = observed.reshape(n, CAP, obs, 1)
    misfit = []
    bias_sum = jnp.zeros((1, 1, 1), jnp.float32)
    for r in range(CAP):
        model = jnp.sum(jac[:, r] * blk_in[:, r : r + 1, :], axis=2, keepdims=True)
        misfit.append(model - o4[:, r])
        bias_sum += jnp.sum(w4[:, r] * misfit[r], axis=(0, 1), keepdims=True)
    bias = bias_sum / weight_sum
    residual = [w4[:, r] * (misfit[r] - bias) for r in range(CAP)]
    for r in range(CAP):
        ret_out[:, r : r + 1, :] = jnp.sum(jac[:, r] * residual[r], axis=1, keepdims=True)
    others(lambda j: remote(ret_out.at[j], ret_in.at[me], 3, j).start())
    ret_in[pl.ds(me, 1)] = ret_out[pl.ds(me, 1)]
    both = jnp.stack(residual, axis=1).reshape(slots, obs, 1)
    res_ref[...] = jnp.sum(both * eye, axis=0)
    scatter_hot = routing((cols * tl, n), 1)
    wait_bytes(ret_in.at[pl.ds(0, n - 1)], recv_sem.at[3])

    start = jnp.dot(
        scatter_hot[0], ret_in[:, 0, :], precision=EXACT, preferred_element_type=jnp.float32
    )
    for r in range(1, CAP):
        start += jnp.dot(
            scatter_hot[r], ret_in[:, r, :], precision=EXACT, preferred_element_type=jnp.float32
        )
    garr[...] = start
    for c in range(cols):
        part = start[c * tl : (c + 1) * tl]
        polar = pack(part[:, 0:LANES], part[:, lat - LANES : lat])
        for t in range(tracers):
            gmsg[:, t * cols + c, :] = polar[t * levels : (t + 1) * levels]
    to_solvers(lambda level, j: remote(gmsg.at[level], gbuf.at[me], 4, j).start())
    to_west = remote(garr, geast, 9, west)
    to_west.start()

    @pl.when(solver)
    def _():
        gbuf[pl.ds(me, 1)] = gmsg[pl.ds(level_here, 1)]
        wait_bytes(gbuf.at[pl.ds(0, n - 1)], recv_sem.at[4])
        g = [[gbuf[:, t * cols + c, :] for c in range(cols)] for t in range(tracers)]
        for step in range(STEPS):
            for t in range(tracers):
                total = sum(g[t][1:], g[t][0])
                mean = jnp.sum(total, axis=0, keepdims=True) / (cols * n)
                row = step * tracers + t
                amout[row : row + 1, :] = mean
                if step == STEPS - 1:
                    continue
                part = [keep_pack * value + w_pack * mean for value in g[t]]
                flux = [pcoef[c, 1] * part[c] for c in range(cols)]
                new = []
                for c in range(cols):
                    from_east = pltpu.roll(flux[0], n - 1, 0) if c == cols - 1 else flux[c + 1]
                    new.append(
                        pcoef[c, 0] * part[c]
                        + from_east
                        + pltpu.roll(pcoef[c, 2] * part[c], 1, 1)
                        + pltpu.roll(pcoef[c, 3] * part[c], LANES - 1, 1)
                    )
                g[t] = new
        ambuf[pl.ds(level_here, 1)] = amout[...][None]
        others(lambda j: remote(amout, ambuf.at[level_here], 5, j).start())

    loads[9].wait()
    to_west.wait_recv()
    wait_solver_blocks(ambuf, recv_sem.at[5])

    group_row = lax.broadcasted_iota(jnp.int32, (group, 1), 0)
    for h in range(tl // group):
        at = lambda c: slice(c * tl + h * group, c * tl + (h + 1) * group)
        g = [garr[at(c), :] for c in range(cols)] + [geast[at(c), :] for c in range(cols)]
        for step in range(STEPS):
            mean = means(ambuf, h, step)
            last = 2 * cols - step
            g = [blend(value, mean, mean) for value in g[:last]]
            new = []
            for c in range(last - 1):
                k = cols + c
                new.append(
                    coef[k, 0] * g[c]
                    + coef[k + 1, 1] * g[c + 1]
                    + pltpu.roll(coef[k, 2] * g[c], 1, 1)
                    + pltpu.roll(coef[k, 3] * g[c], lat - 1, 1)
                )
            g = new
        background = jnp.zeros((group, 1), jnp.float32)
        for i in range(group):
            at_row = h * group + i
            value = bg_ref[at_row // levels, at_row % levels]
            background = jnp.where(group_row == i, value, background)
        for c in range(cols):
            value = background * xarr[at(c), :] + g[c]
            for i in range(2):
                grad_ref[2 * h + i, :, c, :] = value[i * levels : (i + 1) * levels]

    wait_solver_blocks(msg, send_sem.at[0])
    wait_bytes(blk_out.at[pl.ds(0, n - 1)], send_sem.at[2])
    wait_bytes(ret_out.at[pl.ds(0, n - 1)], send_sem.at[3])
    wait_solver_blocks(gmsg, send_sem.at[4])

    @pl.when(solver)
    def _():
        def body(s, carry):
            wait_bytes(mout, send_sem.at[1])
            wait_bytes(amout, send_sem.at[5])
            return carry

        lax.fori_loop(1, n, body, 0)

    to_east.wait_send()
    coef_east.wait_send()
    coef_west.wait_send()
    to_west.wait_send()


def store(*refs):
    sem = refs[6]
    copies = [pltpu.make_async_copy(refs[i], refs[i + 3], sem.at[i]) for i in range(3)]
    for copy in copies:
        copy.start()
    for copy in copies:
        copy.wait()


def shards(
    increment,
    coeffs,
    polar_rows,
    polar_weight,
    block_index,
    send_dest,
    slot_count,
    jacobian,
    observed,
    obs_weight,
    bg_weight,
):
    tracers, levels, cols, lat = increment.shape
    n = lax.axis_size("lon")
    tl = tracers * levels
    obs = jacobian.shape[1]
    sizes = (tl, cols, lat, levels, send_dest.shape[0], polar_rows.shape[0], obs)
    vmem = pl.BlockSpec(memory_space=pltpu.VMEM)
    hbm = pl.BlockSpec(memory_space=pltpu.HBM)
    f32, i32 = jnp.float32, jnp.int32
    field = jax.ShapeDtypeStruct(increment.shape, f32)
    flat = jax.ShapeDtypeStruct((obs, CAP * n), f32)
    rows = (tracers + 3) * cols
    scratch = [
        pltpu.VMEM(increment.shape, f32),
        pltpu.VMEM(coeffs.shape, f32),
        pltpu.SMEM(polar_rows.shape, i32),
        pltpu.SMEM(polar_weight.shape, f32),
        pltpu.SMEM(block_index.shape, i32),
        pltpu.SMEM(send_dest.shape, i32),
        pltpu.SMEM(slot_count.shape, i32),
        pltpu.VMEM((n, CAP, obs, lat), f32),
        pltpu.VMEM(flat.shape, f32),
        pltpu.VMEM(flat.shape, f32),
        pltpu.SMEM(bg_weight.shape, f32),
        pltpu.VMEM((cols * tl, lat), f32),
        pltpu.VMEM((cols * tl, lat), f32),
        pltpu.VMEM(coeffs.shape, f32),
        pltpu.VMEM(coeffs.shape, f32),
        pltpu.VMEM((3 * cols, 4, 2 * levels, lat), f32),
        pltpu.VMEM((levels, rows, LANES), f32),
        pltpu.VMEM((n, rows, LANES), f32),
        pltpu.VMEM((cols, 4, n, LANES), f32),
        pltpu.VMEM((STEPS * tracers, LANES), f32),
        pltpu.VMEM((levels, STEPS * tracers, LANES), f32),
        pltpu.VMEM((cols * tl, lat), f32),
        pltpu.VMEM((n, CAP, lat), f32),
        pltpu.VMEM((n, CAP, lat), f32),
        pltpu.VMEM((n, CAP, lat), f32),
        pltpu.VMEM((n, CAP, lat), f32),
        pltpu.VMEM((cols * tl, lat), f32),
        pltpu.VMEM((cols * tl, lat), f32),
        pltpu.VMEM((levels, tracers * cols, LANES), f32),
        pltpu.VMEM((n, tracers * cols, LANES), f32),
        pltpu.VMEM((STEPS * tracers, LANES), f32),
        pltpu.VMEM((levels, STEPS * tracers, LANES), f32),
        pltpu.SemaphoreType.DMA((10,)),
        pltpu.SemaphoreType.DMA((10,)),
        pltpu.SemaphoreType.DMA((11,)),
    ]
    gradient, model_state, residual = pl.pallas_call(
        functools.partial(kernel, n, sizes),
        out_shape=(field, field, flat),
        in_specs=[hbm] * 11,
        out_specs=(vmem, vmem, vmem),
        scratch_shapes=scratch,
        compiler_params=pltpu.CompilerParams(
            collective_id=0, has_side_effects=True, vmem_limit_bytes=62 * 1024 * 1024
        ),
    )(
        increment,
        coeffs,
        polar_rows,
        polar_weight,
        block_index,
        send_dest,
        slot_count,
        jacobian.reshape(n, CAP, obs, lat),
        observed.T,
        obs_weight.T,
        bg_weight,
    )
    gradient, model_state, residual = pl.pallas_call(
        store,
        out_shape=(field, field, flat),
        in_specs=[hbm] * 3,
        out_specs=(vmem, vmem, vmem),
        scratch_shapes=[pltpu.SemaphoreType.DMA((3,))],
    )(gradient, model_state, residual)
    return gradient, model_state, residual.T


def solution(mesh):
    placed = (
        P(None, None, ("ens", "lon"), None),
        P(None, None, ("ens", "lon"), None),
        P("ens"),
        P("ens"),
        P(("ens", "lon")),
        P(("ens", "lon")),
        P(("ens", "lon")),
        P(("ens", "lon"), None, None),
        P(("ens", "lon"), None),
        P(("ens", "lon"), None),
        P(),
    )
    return jax.shard_map(
        shards,
        mesh=mesh,
        in_specs=placed,
        out_specs=(
            P(None, None, ("ens", "lon"), None),
            P(None, None, ("ens", "lon"), None),
            P(("ens", "lon"), None),
        ),
        check_vma=False,
    )
```
